256 devices in a mesh: row: 32 (over z, x), col: 4 (over y), layer: 2 (over core).
Axes of the slice: x: 4, y: 4, z: 8, core: 2. Of those that a mesh axis runs over, the one named last changes fastest.
Arguments:
- a_blocks: bfloat16 [1024, 32, 72, 72], P('row', ('col', 'layer')), may hold values from -2.5 to 2.5
- a_columns: int32 [1024, 32], P('row', ('col', 'layer')), may hold values from 0 to 1343, as said below
- b_blocks: bfloat16 [1344, 12, 72, 72], P(('row', 'layer'), 'col'), may hold values from -0.75 to 0.75
- b_order: int32 [1344], P(('row', 'layer')), may hold values from 0 to 1343, as said below
- b_columns: int32 [1344, 12], P(('row', 'layer'), 'col'), may hold values from 0 to 167, as said below
- c_columns: int32 [1024, 40], P('row', 'col'), may hold values from 0 to 167, as said below
Outputs:
- product: bfloat16 [1024, 40, 72, 72], P(('row', 'layer'), 'col')
The draws below stay inside these ranges and needn't reach their ends.
Inputs may be any that keep to these rules, and one draw needn't show every extreme that they name: `a_columns`: slot g of a block row names a block column l + 2 * (c * 168 + m) with c = g // 8, l = (g // 4) % 2 and 0 <= m < 168; the 4 slots of one slot group name distinct columns, and all slots of one block row have the same m % 12, the block row's region. `b_order`: A permutation of the 1344 block rows; stored row p holds a block row k with k % 2 == (p // 21) % 2. `b_columns`: each column tile is divided into 12 disjoint sets of 14 block columns, one for each region. Within one stored row and one column tile the 3 columns are distinct and lie in the set of the region (k // 2) % 12 of the stored row's block row k. `c_columns`: within one block row and one column tile the 10 columns are distinct and lie in the set of that tile and of the block row's region.
All inputs are finite; a program needn't handle non-finite values.
Results may differ from the reference program's by a relative error of at most 0.014.
Values may be sent and summed in bfloat16 or wider, within the bound.
No kernel may reach another device: no remote copies, remote signals or barrier semaphores. Data moves between devices by JAX's collectives and lax.ppermute only.
A program may use at most 256 MiB of HBM per device.

```python
import jax
import jax.numpy as jnp
from jax import lax

BS = 72
NB = 1344
BCT = 168
Q = 12
NZA = 4
NZB = 3
NZC = 10
ROWS = 1024
LAYERS = 2
COLS = 4
KP = 168
KBP = 21
N_COL = 4
N_LAYER = 2


def distinct_pick(key, leading, width, pick):
    scores = jax.random.randint(key, (leading, width), 0, 1 << 20) * width + jnp.arange(width, dtype=jnp.int32)[None, :]
    return jnp.argsort(scores, axis=1, stable=True)[:, :pick].astype(jnp.int32)


def spread_pick(key, leading, width, pick, ranks):
    picked = distinct_pick(key, leading, width, pick)
    leading_set = ((jnp.arange(pick, dtype=jnp.int32) - 1) % width).astype(jnp.int32)
    return jnp.where((ranks == 0)[:, None], leading_set[None, :], picked).astype(jnp.int32)


def region_sets(key):
    inner = distinct_pick(jax.random.fold_in(key, 101), N_COL, BCT - 2, BCT - 2) + 1
    first = jnp.zeros((N_COL, 1), jnp.int32)
    final = jnp.full((N_COL, 1), BCT - 1, jnp.int32)
    return jnp.concatenate([first, inner, final], axis=1).astype(jnp.int32).reshape(N_COL, Q, BCT // Q)


def row_regions(key):
    shuffled = distinct_pick(jax.random.fold_in(key, 103), 1, ROWS, ROWS)[0]
    return ((shuffled % Q).astype(jnp.int32), (shuffled // Q).astype(jnp.int32))


def block_order(key):
    per_layer = NB // N_LAYER
    scores = jax.random.randint(jax.random.fold_in(key, 109), (N_LAYER, per_layer), 0, 1 << 20) * per_layer + jnp.arange(per_layer, dtype=jnp.int32)[None, :]
    shuffled = jnp.argsort(scores, axis=1, stable=True).astype(jnp.int32)
    stored = jnp.arange(NB, dtype=jnp.int32)
    layer_ids = stored // KBP % N_LAYER
    within = stored // (KBP * N_LAYER) * KBP + stored % KBP
    return (layer_ids + N_LAYER * shuffled[layer_ids, within]).astype(jnp.int32)


def draw_a_columns(key, part):
    regions, ranks = row_regions(key)
    key = jax.random.fold_in(key, 7)
    groups = N_COL * N_LAYER
    picked = spread_pick(key, ROWS * groups, KP // Q, NZA, jnp.repeat(ranks, groups)).reshape(ROWS, groups, NZA)
    group_ids = jnp.arange(groups, dtype=jnp.int32)
    tile_ids = (group_ids // N_LAYER)[None, :, None]
    layer_ids = (group_ids % N_LAYER)[None, :, None]
    inner = regions[:, None, None] + Q * picked
    return (layer_ids + N_LAYER * (tile_ids * KP + inner)).reshape(ROWS, groups * NZA).astype(jnp.int32)


def draw_b_order(key, part):
    return block_order(key)


def draw_b_columns(key, part):
    order = block_order(key)
    sets = region_sets(key)
    key = jax.random.fold_in(key, 3)
    outer = order // N_LAYER
    regions = outer % Q
    ranks = outer // Q + NB // N_LAYER // Q * (order % N_LAYER)
    picked = spread_pick(key, NB * N_COL, BCT // Q, NZB, jnp.repeat(ranks, N_COL)).reshape(NB, N_COL, NZB)
    tile_ids = jnp.arange(N_COL, dtype=jnp.int32)
    chosen = sets[tile_ids[None, :], regions[:, None]]
    return jnp.take_along_axis(chosen, picked, axis=2).reshape(NB, N_COL * NZB).astype(jnp.int32)


def draw_c_columns(key, part):
    regions, ranks = row_regions(key)
    sets = region_sets(key)
    key = jax.random.fold_in(key, 5)
    picked = spread_pick(key, ROWS * N_COL, BCT // Q, NZC, jnp.repeat(ranks, N_COL)).reshape(ROWS, N_COL, NZC)
    tile_ids = jnp.arange(N_COL, dtype=jnp.int32)
    chosen = sets[tile_ids[None, :], regions[:, None]]
    return jnp.take_along_axis(chosen, picked, axis=2).reshape(ROWS, N_COL * NZC).astype(jnp.int32)


def level_of(rng, shape, pieces, smallest, top_value):
    loudness = 1.0
    for axis_at, blocks in pieces:
        draws = jax.random.uniform(jax.random.fold_in(jax.random.fold_in(rng, 6), axis_at), (blocks,), jnp.float32, smallest / len(pieces), top_value / len(pieces))
        loudness = loudness * jnp.repeat(jnp.exp(draws), shape[axis_at] // blocks).reshape((-1,) + (1,) * (len(shape) - 1 - axis_at))
    return loudness


def normal_values(key, extent, deviation, limit, shards=(), held_as=jnp.bfloat16):
    gain = level_of(key, extent, shards, -0.22, 0.18) if shards else 1.0
    result = jax.random.normal(key, extent, jnp.float32) * deviation * gain
    return jnp.minimum(jnp.maximum(result, -limit), limit).astype(held_as)


def setup_inputs(seed: int = 0) -> dict:
    seeds = jax.random.split(jax.random.key(seed), 7)
    a_blocks = normal_values(seeds[0], (ROWS, COLS * LAYERS * NZA, BS, BS), 0.35, 2.5, ((0, 32), (1, 8)))
    a_columns = draw_a_columns(jax.random.fold_in(seeds[6], 71), 0)
    b_blocks = normal_values(seeds[2], (NB, COLS * NZB, BS, BS), BS ** -0.5, 0.75, ((0, 64), (1, 4)))
    b_order = draw_b_order(jax.random.fold_in(seeds[6], 71), 0)
    b_columns = draw_b_columns(jax.random.fold_in(seeds[6], 71), 0)
    c_columns = draw_c_columns(jax.random.fold_in(seeds[6], 71), 0)
    return dict(a_blocks=a_blocks, a_columns=a_columns, b_blocks=b_blocks, b_order=b_order, b_columns=b_columns, c_columns=c_columns)


def reference(a_blocks, a_columns, b_blocks, b_order, b_columns, c_columns):
    n_slots = a_columns.shape[1]
    n_bslot = b_columns.shape[1]
    n_cslot = c_columns.shape[1]
    position = jnp.zeros((NB,), jnp.int32).at[b_order].set(jnp.arange(NB, dtype=jnp.int32))
    layer_ids = ((jnp.arange(n_slots, dtype=jnp.int32) // NZA) % N_LAYER).astype(jnp.int32)
    b_tiles = (jnp.arange(n_bslot, dtype=jnp.int32) // NZB).astype(jnp.int32)
    c_tiles = (jnp.arange(n_cslot, dtype=jnp.int32) // NZC).astype(jnp.int32)
    c_ids = jnp.arange(n_cslot, dtype=jnp.int32)

    def single_row(operands):
        a_row, column_row, pattern_row = operands
        stored = position[column_row]
        a_square = a_row.astype(jnp.float32)
        b_square = b_blocks[stored].astype(jnp.float32)
        products = jnp.einsum("sab,stbc->stac", a_square, b_square)
        matches = (b_columns[stored][:, :, None] == pattern_row[None, None, :]) & (b_tiles[None, :, None] == c_tiles[None, None, :])
        found_any = jnp.any(matches, axis=2)
        slot_index = jnp.sum(jnp.where(matches, c_ids[None, None, :], 0), axis=2).astype(jnp.int32)
        target = jnp.where(found_any, layer_ids[:, None] * n_cslot + slot_index, N_LAYER * n_cslot).astype(jnp.int32)
        partial_sums = jnp.zeros((N_LAYER * n_cslot, BS, BS), jnp.float32).at[target.reshape(-1)].add(products.reshape(-1, BS, BS), mode="drop")
        rounded = lax.optimization_barrier(partial_sums.astype(jnp.bfloat16)).astype(jnp.float32)
        return jnp.sum(rounded.reshape(N_LAYER, n_cslot, BS, BS), axis=0).astype(jnp.bfloat16)

    return lax.map(single_row, (a_blocks, a_columns, c_columns))
```

```python
import functools

import jax
import jax.numpy as jnp
import numpy as np
from jax import lax
from jax.experimental import pallas as pl
from jax.experimental.pallas import tpu as pltpu
from jax.sharding import PartitionSpec as P

BS = 72
LANES = 128
NZB = 3
NZC = 10
KBP = 21
PAGES = 18
FIRST = 8
REST = PAGES - FIRST
PIECE = 36
USED = NZB * BS
WIDE = NZB * LANES
SLOTS = 16
UNROLL = 4
STEP = 4
PHASES = 3
EARLY = 5
CODE = 1024
NOTE = 64
BASE = 64
NZ, NX = 8, 4
VMEM = 56 * 1024 * 1024


def pack_b_kernel(b_ref, first_ref, rest_ref):
    for j in range(PAGES):
        block, off = j // 2, (j % 2) * PIECE
        page = jnp.concatenate(
            [
                b_ref[j, 0],
                b_ref[j, 1],
                b_ref[j, 2],
                b_ref[PAGES + block // NZB, block % NZB][:, off : off + PIECE],
                jnp.zeros((BS, 2 * LANES - USED - PIECE), jnp.bfloat16),
            ],
            axis=1,
        )
        if j < FIRST:
            first_ref[j] = page
        else:
            rest_ref[j - FIRST] = page


def pack_b(b):
    return pl.pallas_call(
        pack_b_kernel,
        out_shape=[
            jax.ShapeDtypeStruct((FIRST, BS, 2 * LANES), jnp.bfloat16),
            jax.ShapeDtypeStruct((REST, BS, 2 * LANES), jnp.bfloat16),
        ],
        compiler_params=pltpu.CompilerParams(vmem_limit_bytes=16 * 1024 * 1024),
    )(b)


def product_kernel(parts, n_x, n_arrays, first, last, base_ref, count_ref, a_at, b_at, target, a_ref, *refs):
    arrays, refs = refs[:n_arrays], refs[n_arrays:]
    prev, refs = (None, refs) if first else (refs[0], refs[1:])
    outs, refs = (refs[:2], refs[2:]) if last else (refs[:1], refs[1:])
    panel, rows, a_now, acc, done, piece_sems, a_sems, prev_sems, out_sems = refs
    phases = len(parts)
    n_steps = acc.shape[0] // STEP
    n_rows = acc.shape[0]

    def a_copy(at):
        lines = pl.ds(at * STEP, STEP)
        return pltpu.make_async_copy(a_ref.at[lines], a_now.at[lines], a_sems.at[at])

    def prev_copy(at):
        lines = pl.ds(at * STEP, STEP)
        return pltpu.make_async_copy(prev.at[lines], acc.at[lines, pl.ds(0, NZC)], prev_sems.at[at])

    def b_copies(phase):
        found, at = [], 0
        for n, (which, start, size) in enumerate(parts[phase]):
            copy = pltpu.make_async_copy(
                arrays[which].at[pl.ds(start, size)], panel.at[pl.ds(at, size)], piece_sems.at[phase, n]
            )
            found.append((copy, at, size))
            at += size
        return found

    def unpack(page, row, low, high):
        for j in range(low, high):
            p = panel[page + j - low]
            for t in range(NZB):
                rows[row + j, :, t * LANES : t * LANES + BS] = p[:, t * BS : (t + 1) * BS]
        for block in range(low // 2, high // 2):
            two = [panel[page + 2 * block + j - low][:, USED : USED + PIECE] for j in range(2)]
            t = block % NZB
            rows[row + PAGES + block // NZB, :, t * LANES : t * LANES + BS] = jnp.concatenate(two, axis=1)

    def devices(phase):
        return sum(size for _, _, size in parts[phase]) // PAGES

    def unpack_first(n, carry):
        unpack(n * FIRST, n * KBP, 0, FIRST)
        return carry

    def unpack_rest(phase, n, carry):
        n_z = devices(phase) // n_x[phase]
        slot = lax.rem(n, n_z) * n_x[phase] + n // n_z
        unpack(devices(phase) * FIRST + n * REST, slot * KBP, FIRST, PAGES)
        return carry

    def step(phase, k, carry):
        at = lax.rem(k + base_ref[0], n_steps)

        if phase == 0:
            a_copy(at).wait()
        if phase == 0 and not first:
            prev_copy(at).wait()
        for i in range(STEP):
            row = at * STEP + i
            line = phase * n_rows + row
            if phase == 0 and first:
                for u in range(NZC):
                    acc[row, u] = jnp.zeros((BS, LANES), jnp.float32)

            def some(m, carry):
                products = []
                for j in range(UNROLL):
                    pair = line * SLOTS + m * UNROLL + j
                    products.append(
                        jnp.dot(
                            a_now[row, a_at[pair]],
                            rows[b_at[pair]],
                            preferred_element_type=jnp.float32,
                        )
                    )
                for j in range(UNROLL):
                    pair = (line * SLOTS + m * UNROLL + j) * NZB
                    for t in range(NZB):
                        acc[row, target[pair + t]] += products[j][:, t * LANES : (t + 1) * LANES]
                return carry

            lax.fori_loop(0, count_ref[line], some, 0)
            if phase == phases - 1 and last:
                for u in range(NZC):
                    done[k * STEP + i, u] = acc[row, u][:, :BS].astype(jnp.bfloat16)
        if phase == phases - 1 and last:
            half = n_steps // 2

            @pl.when(k < half)
            def _():
                pltpu.make_async_copy(
                    done.at[pl.ds(k * STEP, STEP)], outs[0].at[pl.ds(k * STEP, STEP)], out_sems.at[0]
                ).start()

            @pl.when(k >= half)
            def _():
                pltpu.make_async_copy(
                    done.at[pl.ds(k * STEP, STEP)],
                    outs[1].at[pl.ds((k - half) * STEP, STEP)],
                    out_sems.at[1],
                ).start()
        elif phase == phases - 1:
            lines = pl.ds(at * STEP, STEP)
            pltpu.make_async_copy(
                acc.at[lines, pl.ds(0, NZC)], outs[0].at[lines], out_sems.at[0]
            ).start()
        return carry

    for copy, _, _ in b_copies(0):
        copy.start()
    for at in range(n_steps):
        a_copy(at).start()
        if not first:
            prev_copy(at).start()
    for phase in range(phases):
        for copy, at, size in b_copies(phase):
            copy.wait()
            if at < devices(phase) * FIRST:
                lax.fori_loop(at // FIRST, (at + size) // FIRST, unpack_first, 0)
            else:
                at -= devices(phase) * FIRST
                lax.fori_loop(at // REST, (at + size) // REST, functools.partial(unpack_rest, phase), 0)
        if phase + 1 < phases:
            for copy, _, _ in b_copies(phase + 1):
                copy.start()
        lax.fori_loop(0, n_steps, functools.partial(step, phase), 0)
    if last:
        n = outs[0].shape[0]
        for h, out in enumerate(outs):
            pltpu.make_async_copy(done.at[pl.ds(h * n, n)], out, out_sems.at[h]).wait()
    else:
        pltpu.make_async_copy(acc.at[:, pl.ds(0, NZC)], outs[0], out_sems.at[0]).wait()


def product(base, lists, a, n_rows, arrays, parts, n_x, prev, last):
    count, a_at, b_at, target = [jnp.concatenate(of_phase) for of_phase in zip(*lists)]
    first = prev is None
    n_pages = max(sum(size for _, _, size in part) for part in parts)
    n_devices = n_pages // PAGES
    any_spec = pl.BlockSpec(memory_space=pl.ANY)
    smem = pl.BlockSpec(memory_space=pltpu.SMEM)
    operands = [a, *arrays] + ([] if first else [prev])
    if last:
        out_specs = [any_spec] * 2
        out_shape = [jax.ShapeDtypeStruct((n_rows // 2, NZC, BS, BS), jnp.bfloat16)] * 2
    else:
        out_specs = any_spec
        out_shape = jax.ShapeDtypeStruct((n_rows, NZC, BS, LANES), jnp.float32)
    return pl.pallas_call(
        functools.partial(product_kernel, parts, n_x, len(arrays), first, last),
        in_specs=[smem] * 5 + [any_spec] * len(operands),
        out_specs=out_specs,
        out_shape=out_shape,
        scratch_shapes=[
            pltpu.VMEM((n_pages, BS, 2 * LANES), jnp.bfloat16),
            pltpu.VMEM((n_devices * KBP, BS, WIDE), jnp.bfloat16),
            pltpu.VMEM((n_rows, SLOTS, BS, BS), jnp.bfloat16),
            pltpu.VMEM((n_rows, NZC + 1, BS, LANES), jnp.float32),
            pltpu.VMEM((n_rows if last else 1, NZC, BS, BS), jnp.bfloat16),
            pltpu.SemaphoreType.DMA((len(parts), max(len(p) for p in parts))),
            pltpu.SemaphoreType.DMA((n_rows // STEP,)),
            pltpu.SemaphoreType.DMA((n_rows // STEP,)),
            pltpu.SemaphoreType.DMA((2,)),
        ],
        compiler_params=pltpu.CompilerParams(vmem_limit_bytes=VMEM),
        cost_estimate=pl.CostEstimate(
            flops=len(parts) * 2 * n_rows * SLOTS * BS * BS * WIDE,
            bytes_accessed=len(parts) * n_pages * BS * 512 * 2,
            transcendentals=0,
        ),
    )(base, count, a_at, b_at, target, *operands)


def nothing_kernel(*refs):
    pass


def after(x, *earlier):
    return pl.pallas_call(
        nothing_kernel,
        in_specs=[pl.BlockSpec(memory_space=pl.ANY)] * (1 + len(earlier)),
        out_specs=pl.BlockSpec(memory_space=pl.ANY),
        out_shape=jax.ShapeDtypeStruct(x.shape, x.dtype),
        input_output_aliases={0: 0},
    )(x, *earlier)


def along_x(x, d):
    return lax.ppermute(x, "row", [(z * NX + k, z * NX + (k + d) % NX) for z in range(NZ) for k in range(NX)])


def along_z(x, d):
    return lax.ppermute(x, "row", [(z * NX + k, (z + d) % NZ * NX + k) for z in range(NZ) for k in range(NX)])


def along_col(x, d):
    n = lax.axis_size("col")
    return lax.ppermute(x, "col", [(k, (k + d) % n) for k in range(n)])


def both_ways(move, x, n):
    got, up, down = [], x, x
    for _ in range(n // 2 - 1):
        up, down = move(up, 1), move(down, -1)
        got += [up, down]
    h = x.shape[0] // 2
    return got, [move(up[:h], 1), move(down[h:], -1)]


def place_table():
    table = np.zeros((NZ, NX), np.int32)
    for i, z in enumerate((0, -1, 1, -2, 2, -3, 3, 4)):
        for j, x in enumerate((0, -1, 1, 2)):
            near = j < NX - 1
            phase = (0 if i < EARLY else 1) if near else 2
            slot = (i if i < EARLY else i - EARLY) * (NX - 1) + j if near else i
            table[z % NZ, x % NX] = phase * CODE + slot * KBP
    return table


def on_device(a_blocks, a_columns, b_blocks, b_order, b_columns, c_columns):
    rows = a_blocks.shape[0]

    note = jnp.concatenate([b_order, b_columns.reshape(-1)])
    note = jnp.pad(note, (0, NOTE * LANES - note.shape[0])).reshape(NOTE, LANES)
    notes = lax.all_gather(note, "row", axis=0, tiled=True).reshape(NZ * NX, NOTE * LANES)

    digits = jnp.stack([a_columns // BASE, a_columns % BASE]).astype(jnp.bfloat16)
    own = jnp.pad(digits.reshape(2 * rows, NZB + 1).T[:, None, :], ((0, 0), (0, BS - 1), (0, BS - 2 * rows)))
    a_own = jnp.concatenate([a_blocks, own[None]], axis=0)
    a_got = [along_col(a_own, 1), along_col(a_own, -1)]

    first, rest = pack_b(b_blocks)
    got, halves = both_ways(along_x, first, NX)
    column = jnp.concatenate([first] + got + halves, axis=0)
    got, halves = both_ways(along_z, rest, NZ)
    line = jnp.concatenate([rest] + got + halves, axis=0)
    l_got, l_halves = both_ways(along_x, line, NX)
    column = after(column, *halves)
    half_a = (rows + 1) // 2
    a_halves = [along_col(after(a_got[0][:half_a], *halves), 1), along_col(after(a_got[1][half_a:], *halves), -1)]
    c_got = [along_z(column, 1), along_z(column, -1)]
    c_got += [along_z(c_got[0], 1), along_z(c_got[1], -1)]
    c_got[2] = after(c_got[2], *a_halves)
    c_got += [along_z(c_got[2], 1), along_z(c_got[3], -1)]
    half_c, half = column.shape[0] // 2, line.shape[0] // 2
    c_halves = [along_z(c_got[4][:half_c], 1), along_z(c_got[5][half_c:], -1)]

    a = jnp.concatenate([a_own] + a_got + [jnp.concatenate(a_halves, axis=0)], axis=1)
    digits = a[rows, :, 0, : 2 * rows].astype(jnp.float32).astype(jnp.int32).reshape(SLOTS, 2, rows)
    wanted = (digits[:, 0] * BASE + digits[:, 1]).T

    near, cut = 3 * FIRST, EARLY * REST
    arrays = [column] + c_got[:4] + [line] + l_got
    parts = [[(n, 0, near) for n in range(EARLY)] + [(EARLY + n, 0, cut) for n in range(3)]]
    late_arrays = [column] + c_got + c_halves + [line] + l_got + l_halves
    at = NZ + 1
    late_parts = [
        [(n, 0, near) for n in range(EARLY, NZ - 1)]
        + [(NZ - 1, 0, half_c), (NZ, 0, near - half_c)]
        + [(at + n, cut, line.shape[0] - cut) for n in range(3)],
        [(n, near, FIRST) for n in range(NZ - 1)]
        + [(NZ, near - half_c, FIRST)]
        + [(at + 3, 0, half), (at + 4, 0, half)],
    ]

    order = notes[:, :KBP].reshape(-1)
    columns_b = notes[:, KBP : KBP * (1 + NZB)].reshape(-1, NZB)
    row_at = lax.axis_index("row").astype(jnp.int32)
    device = jnp.arange(NZ * NX, dtype=jnp.int32)
    apart = (device // NX - row_at // NX) % NZ * NX + (device % NX - row_at % NX) % NX
    table = place_table()[:, :, None] + np.arange(KBP)
    table = jnp.asarray(table.reshape(NZ * NX, KBP), jnp.int32)
    place = apart[:, None] == device[None, :]
    codes = jnp.sum(jnp.where(place[:, :, None], table[None], 0), axis=1).reshape(-1)
    same = wanted.reshape(-1, 1) == order[None, :]

    def look_up(values):
        return jnp.sum(jnp.where(same, values[None, :], 0), axis=1).reshape(rows, SLOTS)

    code = look_up(codes)
    slot_ids = jnp.arange(NZC, dtype=jnp.int32)
    targets = []
    for t in range(NZB):
        match = look_up(columns_b[:, t])[:, :, None] == c_columns[:, None, :]
        targets.append(jnp.sum(jnp.where(match, slot_ids - NZC, 0), axis=2))
    chunk, place = code // CODE, code % CODE
    slots = jnp.arange(SLOTS, dtype=jnp.int32)
    lists = []
    for c in range(PHASES):
        mine = chunk == c
        upto = (slots[:, None] <= slots[None, :])[None]
        rank = jnp.sum(jnp.where(upto & mine[:, :, None], 1, 0), axis=1) - 1
        chosen = mine[:, None, :] & (rank[:, None, :] == slots[None, :, None])

        def listed(values):
            return jnp.sum(jnp.where(chosen, values[:, None, :], 0), axis=2)

        count = (jnp.sum(jnp.where(mine, 1, 0), axis=1) + UNROLL - 1) // UNROLL
        target = jnp.stack([listed(v) for v in targets], axis=2) + NZC
        a_at = listed(jnp.broadcast_to(slots[None, :], mine.shape))
        lists.append((count, a_at.reshape(-1), listed(place).reshape(-1), target.reshape(-1)))

    me = lax.axis_index("layer").astype(jnp.int32)
    base = ((1 - me) * (rows // 2 // STEP)).reshape(1)
    part = product(base, lists[:1], a, rows, arrays, parts, (NX - 1,), None, False)
    sent, kept = product(base, lists[1:], a, rows, late_arrays, late_parts, (NX - 1, 1), part, True)
    got = lax.ppermute(sent, "layer", [(0, 1), (1, 0)])
    return (kept.astype(jnp.float32) + got.astype(jnp.float32)).astype(jnp.bfloat16)


def solution(mesh):
    in_specs = (
        P("row", ("col", "layer"), None, None),
        P("row", ("col", "layer")),
        P(("row", "layer"), "col", None, None),
        P(("row", "layer")),
        P(("row", "layer"), "col"),
        P("row", "col"),
    )
    out_specs = P(("row", "layer"), "col", None, None)
    return jax.shard_map(
        on_device, mesh=mesh, in_specs=in_specs, out_specs=out_specs, check_vma=False
    )
```

```python
import functools

import jax
import jax.numpy as jnp
from jax import lax
from jax.experimental import pallas as pl
from jax.experimental.pallas import tpu as pltpu
from jax.sharding import PartitionSpec as P

BS = 72
LANES = 128
NZB = 3
NZC = 10
KBP = 21
PAGES = 18
EXTRA = KBP - PAGES
PER = PAGES // EXTRA
PIECE = NZB * BS // PER
USED = NZB * BS
SLOTS = 16
VMEM = 48 * 1024 * 1024


def pack_b_kernel(b_ref, out_ref):
    for r in range(PAGES):
        e, j = PAGES + r // PER, r % PER
        lane = j * PIECE
        t, off = lane // BS, lane % BS
        out_ref[r] = jnp.concatenate(
            [
                b_ref[r, 0],
                b_ref[r, 1],
                b_ref[r, 2],
                b_ref[e, t][:, off : off + PIECE],
                jnp.zeros((BS, 2 * LANES - USED - PIECE), jnp.bfloat16),
            ],
            axis=1,
        )


def pack_b(b):
    return pl.pallas_call(
        pack_b_kernel,
        out_shape=jax.ShapeDtypeStruct((PAGES, BS, 2 * LANES), jnp.bfloat16),
        compiler_params=pltpu.CompilerParams(vmem_limit_bytes=VMEM),
    )(b)


def extra_kernel(p_ref, out_ref):
    lo = USED - LANES
    for e in range(EXTRA):
        pieces = [p_ref[e * PER + j][:, lo : lo + PIECE] for j in range(PER)]
        pieces.append(jnp.zeros((BS, 2 * LANES - USED), jnp.bfloat16))
        out_ref[e] = jnp.concatenate(pieces, axis=1)


def extra_rows(panel):
    devices = panel.shape[0] // PAGES
    return pl.pallas_call(
        extra_kernel,
        grid=(devices,),
        in_specs=[pl.BlockSpec((PAGES, BS, LANES), lambda i: (i, 0, 1))],
        out_specs=pl.BlockSpec((EXTRA, BS, 2 * LANES), lambda i: (i, 0, 0)),
        out_shape=jax.ShapeDtypeStruct((devices * EXTRA, BS, 2 * LANES), jnp.bfloat16),
    )(panel)


def product_kernel(
    base_ref, page_ref, target_ref, a0, a1, a2, a3, panel, extra, out_ref, pages, acc, sems
):
    step = pl.program_id(0)
    steps = pl.num_programs(0)
    n_panel = panel.shape[0]

    def fetch(at):
        slot = lax.rem(at, 2)
        first = (base_ref[0] + at) * SLOTS
        for g in range(SLOTS):
            page = page_ref[first + g]

            @pl.when(page < n_panel)
            def _():
                pltpu.make_async_copy(panel.at[page], pages.at[slot, g], sems.at[slot]).start()

            @pl.when(page >= n_panel)
            def _():
                pltpu.make_async_copy(
                    extra.at[page - n_panel], pages.at[slot, g], sems.at[slot]
                ).start()

    @pl.when(step == 0)
    def _():
        fetch(step)

    @pl.when(step + 1 < steps)
    def _():
        fetch(step + 1)

    acc[...] = jnp.zeros_like(acc)
    slot = lax.rem(step, 2)
    pltpu.make_async_copy(panel.at[pl.ds(0, SLOTS)], pages.at[slot], sems.at[slot]).wait()
    first = (base_ref[0] + step) * SLOTS
    for g in range(SLOTS):
        a = (a0, a1, a2, a3)[g // 4][0, g % 4]
        r = jnp.dot(a, pages[slot, g], preferred_element_type=jnp.float32)
        lo, hi = r[:, :LANES], r[:, LANES:]
        at = (first + g) * NZB
        u0, u1, u2 = target_ref[at], target_ref[at + 1], target_ref[at + 2]
        acc[0, u0] += lo
        acc[1, u1] += lo
        acc[2, u1] += hi
        acc[3, u2] += hi
    cut = LANES - BS
    for u in range(NZC):
        c0 = acc[0, u][:, :BS]
        c1 = jnp.concatenate([acc[1, u][:, BS:], acc[2, u][:, : BS - cut]], axis=1)
        c2 = acc[3, u][:, BS - cut : 2 * BS - cut]
        out_ref[0, u] = (c0 + c1 + c2).astype(out_ref.dtype)


def product(base, page, target, a_parts, panel, extra, rows):
    a_spec = pl.BlockSpec((1, 4, BS, BS), lambda i, base, page, target: (base[0] + i, 0, 0, 0))
    any_spec = pl.BlockSpec(memory_space=pl.ANY)
    grid_spec = pltpu.PrefetchScalarGridSpec(
        num_scalar_prefetch=3,
        grid=(rows,),
        in_specs=[a_spec] * 4 + [any_spec] * 2,
        out_specs=pl.BlockSpec((1, NZC, BS, BS), lambda i, *_: (i, 0, 0, 0)),
        scratch_shapes=[
            pltpu.VMEM((2, SLOTS, BS, 2 * LANES), jnp.bfloat16),
            pltpu.VMEM((4, NZC + 1, BS, LANES), jnp.float32),
            pltpu.SemaphoreType.DMA((2,)),
        ],
    )
    return pl.pallas_call(
        product_kernel,
        grid_spec=grid_spec,
        out_shape=jax.ShapeDtypeStruct((rows, NZC, BS, BS), jnp.bfloat16),
        compiler_params=pltpu.CompilerParams(vmem_limit_bytes=VMEM),
        cost_estimate=pl.CostEstimate(
            flops=2 * rows * SLOTS * BS * BS * 256,
            bytes_accessed=rows * SLOTS * BS * 512,
            transcendentals=0,
        ),
    )(base, page, target, *a_parts, panel, extra)


def around(axis, n, d):
    return functools.partial(lax.ppermute, axis_name=axis, perm=[(k, (k + d) % n) for k in range(n)])


def on_device(a_blocks, a_columns, b_blocks, b_order, b_columns, c_columns):
    rows = a_blocks.shape[0]
    n_col = lax.axis_size("col")
    panel = lax.all_gather(pack_b(b_blocks), "row", axis=0, tiled=True)

    a_parts, column_parts = [a_blocks], [a_columns]
    for d in range(1, n_col):
        a_parts.append(around("col", n_col, d)(a_blocks))
        column_parts.append(around("col", n_col, d)(a_columns))

    notes = jnp.concatenate([b_order, b_columns.reshape(-1)])[None]
    notes = lax.all_gather(notes, "row", axis=0, tiled=True)
    order = notes[:, :KBP].reshape(-1)
    columns_b = notes[:, KBP:].reshape(-1, NZB)
    wanted = jnp.concatenate(column_parts, axis=1).reshape(-1, 1)
    same = wanted == order[None, :]
    stored_ids = jnp.arange(order.shape[0], dtype=jnp.int32)
    stored = jnp.sum(jnp.where(same, stored_ids[None, :], 0), axis=1)
    device, row = stored // KBP, stored % KBP
    n_panel = panel.shape[0]
    page = jnp.where(row < PAGES, device * PAGES + row, n_panel + device * EXTRA + row - PAGES)
    targets = []
    for t in range(NZB):
        column = jnp.sum(jnp.where(same, columns_b[:, t][None, :], 0), axis=1).reshape(rows, SLOTS)
        match = column[:, :, None] == c_columns[:, None, :]
        slot_ids = jnp.arange(NZC, dtype=jnp.int32)
        slot = jnp.sum(jnp.where(match, slot_ids, 0), axis=2)
        targets.append(jnp.where(jnp.any(match, axis=2), slot, NZC))
    target = jnp.stack(targets, axis=2).reshape(-1).astype(jnp.int32)

    extra = extra_rows(panel)
    half = rows // 2
    me = lax.axis_index("layer").astype(jnp.int32)
    run = functools.partial(product, page=page, target=target, a_parts=a_parts, panel=panel, extra=extra, rows=half)
    sent = run(((1 - me) * half).reshape(1))
    got = lax.ppermute(sent, "layer", [(0, 1), (1, 0)])
    kept = run((me * half).reshape(1))
    return (kept.astype(jnp.float32) + got.astype(jnp.float32)).astype(jnp.bfloat16)


def solution(mesh):
    in_specs = (
        P("row", ("col", "layer"), None, None),
        P("row", ("col", "layer")),
        P(("row", "layer"), "col", None, None),
        P(("row", "layer")),
        P(("row", "layer"), "col"),
        P("row", "col"),
    )
    out_specs = P(("row", "layer"), "col", None, None)
    return jax.shard_map(
        on_device, mesh=mesh, in_specs=in_specs, out_specs=out_specs, check_vma=False
    )
```

```python
import functools

import jax
import jax.numpy as jnp
from jax import lax
from jax.experimental import pallas as pl
from jax.experimental.pallas import tpu as pltpu
from jax.sharding import PartitionSpec as P

BS = 72
LANES = 128
NZB = 3
NZC = 10
KBP = 21
PAGES = 18
EXTRA = KBP - PAGES
PER = PAGES // EXTRA
PIECE = NZB * BS // PER
USED = NZB * BS
SLOTS = 16
TOGETHER = 4
VMEM = 48 * 1024 * 1024


def pack_b_kernel(b_ref, out_ref):
    for r in range(PAGES):
        e, j = PAGES + r // PER, r % PER
        lane = j * PIECE
        t, off = lane // BS, lane % BS
        out_ref[r] = jnp.concatenate(
            [
                b_ref[r, 0],
                b_ref[r, 1],
                b_ref[r, 2],
                b_ref[e, t][:, off : off + PIECE],
                jnp.zeros((BS, 2 * LANES - USED - PIECE), jnp.bfloat16),
            ],
            axis=1,
        )


def pack_b(b):
    return pl.pallas_call(
        pack_b_kernel,
        out_shape=jax.ShapeDtypeStruct((PAGES, BS, 2 * LANES), jnp.bfloat16),
        compiler_params=pltpu.CompilerParams(vmem_limit_bytes=VMEM),
    )(b)


def extra_kernel(p_ref, out_ref):
    lo = USED - LANES
    for e in range(out_ref.shape[0]):
        for t in range(NZB):
            two = [p_ref[e * PER + 2 * t + j][:, lo : lo + PIECE] for j in range(2)]
            out_ref[e, :, t * BS : (t + 1) * BS] = jnp.concatenate(two, axis=1)
        out_ref[e, :, USED:] = jnp.zeros((BS, 2 * LANES - USED), jnp.bfloat16)


def extra_rows(panel):
    devices = panel.shape[0] // PAGES
    return pl.pallas_call(
        extra_kernel,
        grid=(devices // TOGETHER,),
        in_specs=[pl.BlockSpec((TOGETHER * PAGES, BS, LANES), lambda i: (i, 0, 1))],
        out_specs=pl.BlockSpec((TOGETHER * EXTRA, BS, 2 * LANES), lambda i: (i, 0, 0)),
        out_shape=jax.ShapeDtypeStruct((devices * EXTRA, BS, 2 * LANES), jnp.bfloat16),
        compiler_params=pltpu.CompilerParams(vmem_limit_bytes=VMEM),
    )(panel)


def product_kernel(
    base_ref, page_ref, target_ref, a0, a1, a2, a3, panel, extra, out_ref, pages, acc, sems
):
    step = pl.program_id(0)
    steps = pl.num_programs(0)
    n_panel = panel.shape[0]

    def fetch(at):
        slot = lax.rem(at, 2)
        first = (base_ref[0] + at) * SLOTS
        for g in range(SLOTS):
            page = page_ref[first + g]

            @pl.when(page < n_panel)
            def _():
                pltpu.make_async_copy(panel.at[page], pages.at[slot, g], sems.at[slot]).start()

            @pl.when(page >= n_panel)
            def _():
                pltpu.make_async_copy(
                    extra.at[page - n_panel], pages.at[slot, g], sems.at[slot]
                ).start()

    @pl.when(step == 0)
    def _():
        fetch(step)

    @pl.when(step + 1 < steps)
    def _():
        fetch(step + 1)

    acc[...] = jnp.zeros_like(acc)
    slot = lax.rem(step, 2)
    pltpu.make_async_copy(panel.at[pl.ds(0, SLOTS)], pages.at[slot], sems.at[slot]).wait()
    first = (base_ref[0] + step) * SLOTS
    for g in range(SLOTS):
        a = (a0, a1, a2, a3)[g // 4][0, g % 4]
        r = jnp.dot(a, pages[slot, g], preferred_element_type=jnp.float32)
        lo, hi = r[:, :LANES], r[:, LANES:]
        at = (first + g) * NZB
        u0, u1, u2 = target_ref[at], target_ref[at + 1], target_ref[at + 2]
        acc[0, u0] += lo
        acc[1, u1] += lo
        acc[2, u1] += hi
        acc[3, u2] += hi
    cut = LANES - BS
    for u in range(NZC):
        c0 = acc[0, u][:, :BS]
        c1 = jnp.concatenate([acc[1, u][:, BS:], acc[2, u][:, : BS - cut]], axis=1)
        c2 = acc[3, u][:, BS - cut : 2 * BS - cut]
        out_ref[0, u] = (c0 + c1 + c2).astype(out_ref.dtype)


def product(base, page, target, a_parts, panel, extra, rows):
    a_spec = pl.BlockSpec((1, 4, BS, BS), lambda i, base, page, target: (base[0] + i, 0, 0, 0))
    any_spec = pl.BlockSpec(memory_space=pl.ANY)
    grid_spec = pltpu.PrefetchScalarGridSpec(
        num_scalar_prefetch=3,
        grid=(rows,),
        in_specs=[a_spec] * 4 + [any_spec] * 2,
        out_specs=pl.BlockSpec((1, NZC, BS, BS), lambda i, *_: (i, 0, 0, 0)),
        scratch_shapes=[
            pltpu.VMEM((2, SLOTS, BS, 2 * LANES), jnp.bfloat16),
            pltpu.VMEM((4, NZC + 1, BS, LANES), jnp.float32),
            pltpu.SemaphoreType.DMA((2,)),
        ],
    )
    return pl.pallas_call(
        product_kernel,
        grid_spec=grid_spec,
        out_shape=jax.ShapeDtypeStruct((rows, NZC, BS, BS), jnp.bfloat16),
        compiler_params=pltpu.CompilerParams(vmem_limit_bytes=VMEM),
        cost_estimate=pl.CostEstimate(
            flops=2 * rows * SLOTS * BS * BS * 256,
            bytes_accessed=rows * SLOTS * BS * 512,
            transcendentals=0,
        ),
    )(base, page, target, *a_parts, panel, extra)


def around(axis, n, d):
    return functools.partial(lax.ppermute, axis_name=axis, perm=[(k, (k + d) % n) for k in range(n)])


def on_device(a_blocks, a_columns, b_blocks, b_order, b_columns, c_columns):
    rows = a_blocks.shape[0]
    n_col = lax.axis_size("col")
    panel = lax.all_gather(pack_b(b_blocks), "row", axis=0, tiled=True)

    a_parts, column_parts = [a_blocks], [a_columns]
    for d in range(1, n_col):
        a_parts.append(around("col", n_col, d)(a_blocks))
        column_parts.append(around("col", n_col, d)(a_columns))

    notes = jnp.concatenate([b_order, b_columns.reshape(-1)])[None]
    notes = lax.all_gather(notes, "row", axis=0, tiled=True)
    order = notes[:, :KBP].reshape(-1)
    columns_b = notes[:, KBP:].reshape(-1, NZB)
    wanted = jnp.concatenate(column_parts, axis=1).reshape(-1, 1)
    same = wanted == order[None, :]
    stored_ids = jnp.arange(order.shape[0], dtype=jnp.int32)
    stored = jnp.sum(jnp.where(same, stored_ids[None, :], 0), axis=1)
    device, row = stored // KBP, stored % KBP
    n_panel = panel.shape[0]
    page = jnp.where(row < PAGES, device * PAGES + row, n_panel + device * EXTRA + row - PAGES)
    targets = []
    for t in range(NZB):
        column = jnp.sum(jnp.where(same, columns_b[:, t][None, :], 0), axis=1).reshape(rows, SLOTS)
        match = column[:, :, None] == c_columns[:, None, :]
        slot_ids = jnp.arange(NZC, dtype=jnp.int32)
        slot = jnp.sum(jnp.where(match, slot_ids, 0), axis=2)
        targets.append(jnp.where(jnp.any(match, axis=2), slot, NZC))
    target = jnp.stack(targets, axis=2).reshape(-1).astype(jnp.int32)

    extra = extra_rows(panel)
    half = rows // 2
    me = lax.axis_index("layer").astype(jnp.int32)
    run = functools.partial(product, page=page, target=target, a_parts=a_parts, panel=panel, extra=extra, rows=half)
    sent = run(((1 - me) * half).reshape(1))
    got = lax.ppermute(sent, "layer", [(0, 1), (1, 0)])
    kept = run((me * half).reshape(1))
    return (kept.astype(jnp.float32) + got.astype(jnp.float32)).astype(jnp.bfloat16)


def solution(mesh):
    in_specs = (
        P("row", ("col", "layer"), None, None),
        P("row", ("col", "layer")),
        P(("row", "layer"), "col", None, None),
        P(("row", "layer")),
        P(("row", "layer"), "col"),
        P("row", "col"),
    )
    out_specs = P(("row", "layer"), "col", None, None)
    return jax.shard_map(
        on_device, mesh=mesh, in_specs=in_specs, out_specs=out_specs, check_vma=False
    )
```
